32 devices in a mesh: groups: 2 (over y), row: 4 (over z), col: 4 (over x, core).
Axes of the slice: x: 2, y: 2, z: 4, core: 2. Of those that a mesh axis runs over, the one named last changes fastest.
Arguments:
- pair_state: bfloat16 [160, 80, 128], P(('groups', 'row'), 'col'), parts along dimension 0, may hold values from -6 to 6
- token_mask: int32 [160], P('groups'), parts along dimension 0, may hold values 0 or 1
- norm_gain: float32 [128], replicated, may hold values from 0.1 to 1.9
- norm_bias: float32 [128], replicated, may hold values from -3 to 3
- proj_weight: bfloat16 [128, 512], replicated, may hold values from -0.5 to 0.5
- gate_weight: bfloat16 [128, 128], replicated, may hold values from -0.5 to 0.5
- tri_gain: float32 [128], replicated, may hold values from 0.1 to 1.9
- tri_bias: float32 [128], replicated, may hold values from -3 to 3
- out_weight: bfloat16 [128, 128], replicated, may hold values from -0.5 to 0.5
- trans_gain: float32 [128], replicated, may hold values from 0.1 to 1.9
- trans_bias: float32 [128], replicated, may hold values from -3 to 3
- trans_in: bfloat16 [128, 1024], replicated, may hold values from -0.5 to 0.5
- trans_out: bfloat16 [512, 128], replicated, may hold values from -0.25 to 0.25
Outputs:
- pair_columns: bfloat16 [160, 4, 20, 128], P('groups', 'col', 'row'), parts along dimension 0
The draws below stay inside these ranges and needn't reach their ends.
There are 2 independent parts, one for each index of `groups`. The reference program is written for one: setup_inputs(seed, part) draws one part's arguments, and reference() takes and returns one part's arrays. A program takes and returns all parts, laid end to end along the dimension named above; an argument that names none is the same for every part. Nothing has to cross between parts.
All inputs are finite; a program needn't handle non-finite values.
Results may differ from the reference program's by a relative error of at most 0.0062.
Values may be sent and summed in bfloat16 or wider, within the bound.
A program may use at most 128 MiB of HBM per device.

```python
import jax
import jax.numpy as jnp
from jax import lax

C = 128
CH = 128
EXPAND = 4
N = 80
N_ROW = 4
N_COL = 4


def with_ends(values, key, smallest, high):
    spot = [jax.random.randint(jax.random.fold_in(key, axis), (), 0, length) for axis, length in enumerate(values.shape)]
    longest = values.shape.index(max(values.shape))
    beside = spot[:longest] + [(spot[longest] + 1) % values.shape[longest]] + spot[longest + 1:]
    return values.at[tuple(spot)].set(smallest).at[tuple(beside)].set(high)


def level_of(rng, shape, shards, least, largest):
    level, own = 1.0, jax.random.fold_in(rng, 6)
    for position, shards_of in shards:
        steps = jnp.exp(jax.random.uniform(jax.random.fold_in(own, position), (shards_of,), jnp.float32, least / len(shards), largest / len(shards)))
        level = level * jnp.repeat(steps, shape[position] // shards_of).reshape([-1 if axis == position else 1 for axis in range(len(shape))])
    return level


def centred(stream_key, shape, deviation, reach, cuts=(), dtype=jnp.bfloat16):
    factor_of = level_of(stream_key, shape, cuts, -0.22, 0.18) if cuts else 1.0
    array = jax.random.normal(stream_key, shape, jnp.float32) * deviation * factor_of
    return jnp.minimum(jnp.maximum(array, -reach), reach).astype(dtype)


def setup_inputs(seed: int = 0, part: int = 0) -> dict:
    streams_of = jax.random.split(jax.random.key(seed), 14)
    part_keys = jax.random.split(jax.random.fold_in(streams_of[13], part), 14)
    pair_state = centred(part_keys[0], (N, N, C), 1.0, 6.0, ((0, 4), (1, 4)))
    token_mask = with_ends((jax.random.randint(part_keys[1], (N,), 0, 8) < 7).astype(jnp.int32), jax.random.fold_in(part_keys[1], 1), 0, 1)
    norm_gain = jnp.clip(1.0 + 0.18 * jax.random.normal(streams_of[2], (C,), jnp.float32), 0.1, 1.9)
    norm_bias = centred(streams_of[3], (C,), 0.5, 3.0, (), jnp.float32)
    proj_weight = centred(streams_of[4], (C, 4 * CH), C ** -0.5, 0.5)
    gate_weight = centred(streams_of[5], (C, C), C ** -0.5, 0.5)
    tri_gain = jnp.clip(1.0 + 0.18 * jax.random.normal(streams_of[6], (CH,), jnp.float32), 0.1, 1.9)
    tri_bias = centred(streams_of[7], (CH,), 0.5, 3.0, (), jnp.float32)
    out_weight = centred(streams_of[8], (CH, C), CH ** -0.5, 0.5)
    trans_gain = jnp.clip(1.0 + 0.18 * jax.random.normal(streams_of[9], (C,), jnp.float32), 0.1, 1.9)
    trans_bias = centred(streams_of[10], (C,), 0.5, 3.0, (), jnp.float32)
    trans_in = centred(streams_of[11], (C, 2 * EXPAND * C), C ** -0.5, 0.5)
    trans_out = centred(streams_of[12], (EXPAND * C, C), (EXPAND * C) ** -0.5, 0.25)
    return dict(pair_state=pair_state, token_mask=token_mask, norm_gain=norm_gain, norm_bias=norm_bias, proj_weight=proj_weight, gate_weight=gate_weight, tri_gain=tri_gain, tri_bias=tri_bias, out_weight=out_weight, trans_gain=trans_gain, trans_bias=trans_bias, trans_in=trans_in, trans_out=trans_out)


epsilon = 1e-05

def layer_norm(values, gain, bias):
    center = lax.optimization_barrier(jnp.mean(values, axis=-1, keepdims=True))
    spread = lax.optimization_barrier(jnp.mean(jnp.square(values - center), axis=-1, keepdims=True))
    return (values - center) * lax.rsqrt(spread + epsilon) * gain + bias

def reference(pair_state, token_mask, norm_gain, norm_bias, proj_weight, gate_weight, tri_gain, tri_bias, out_weight, trans_gain, trans_bias, trans_in, trans_out):
    weights = token_mask.astype(jnp.float32)
    row_blocks = pair_state.reshape(N_ROW, N // N_ROW, N, C)
    weight_blocks = weights.reshape(N_ROW, N // N_ROW)

    def normalize(item_block):
        return layer_norm(item_block.astype(jnp.float32), norm_gain, norm_bias).astype(jnp.bfloat16)

    def project(inputs):
        item_block, row_weight = inputs
        normed = normalize(item_block)
        projected = jnp.dot(normed.reshape(-1, C), proj_weight, preferred_element_type=jnp.float32)
        projected = projected.reshape(N // N_ROW, N, 4 * CH)
        pair_weight = (row_weight[:, None] * weights[None, :])[:, :, None]
        left_panel = (pair_weight * jax.nn.sigmoid(projected[..., CH:2 * CH]) * projected[..., :CH]).astype(jnp.bfloat16)
        right_panel = (pair_weight * jax.nn.sigmoid(projected[..., 3 * CH:]) * projected[..., 2 * CH:3 * CH]).astype(jnp.bfloat16)
        return (left_panel, right_panel)
    left_all, right_all = lax.map(project, (row_blocks, weight_blocks))
    right_full = right_all.reshape(N, N, CH).astype(jnp.float32)

    def finish(inputs):
        item_block, left_block = inputs
        triangle = jnp.einsum('ikc,jkc->ijc', left_block.astype(jnp.float32), right_full)
        tri_normed = layer_norm(triangle, tri_gain, tri_bias).astype(jnp.bfloat16)
        branch = jnp.dot(tri_normed.reshape(-1, CH), out_weight, preferred_element_type=jnp.float32)
        normed = normalize(item_block).reshape(-1, C)
        gate_value = jax.nn.sigmoid(jnp.dot(normed, gate_weight, preferred_element_type=jnp.float32))
        updated = (item_block.reshape(-1, C).astype(jnp.float32) + gate_value * branch).astype(jnp.bfloat16)
        trans_normed = layer_norm(updated.astype(jnp.float32), trans_gain, trans_bias).astype(jnp.bfloat16)
        hidden_act = jnp.dot(trans_normed, trans_in, preferred_element_type=jnp.float32)
        activated = (jax.nn.silu(hidden_act[:, :EXPAND * C]) * hidden_act[:, EXPAND * C:]).astype(jnp.bfloat16)
        result = updated.astype(jnp.float32) + jnp.dot(activated, trans_out, preferred_element_type=jnp.float32)
        return result.astype(jnp.bfloat16).reshape(N // N_ROW, N, C)
    finished = lax.map(finish, (row_blocks, left_all))
    return finished.reshape(N, N_COL, N // N_COL, C)
```

```python
import functools

import jax
import jax.numpy as jnp
from jax import lax
from jax.experimental import pallas as pl
from jax.experimental.pallas import tpu as pltpu
from jax.sharding import PartitionSpec as P

epsilon = 1e-05
MESH = pl.DeviceIdType.MESH
f32 = jnp.float32
bf16 = jnp.bfloat16


def layer_norm(values, gain, bias):
    center = jnp.mean(values, axis=-1, keepdims=True)
    moved = values - center
    spread = jnp.mean(jnp.square(moved), axis=-1, keepdims=True)
    return moved * lax.rsqrt(spread + epsilon) * gain + bias


def sigmoid(values):
    return 0.5 * jnp.tanh(0.5 * values) + 0.5


def chunk_of(total):
    return max(size for size in range(16, 513, 16) if total % size == 0)


def nearest(me, step, count):
    ends = jnp.minimum(me, count - 1 - me)
    between = jnp.where(step % 2 == 1, me + (step + 1) // 2, me - step // 2)
    outside = jnp.where(me <= count - 1 - me, step, count - 1 - step)
    return jnp.where(step <= 2 * ends, between, outside)


def kernel(
    n_row, n_col,
    pair_ref, mask_ref, norm_gain, norm_bias, proj_ref, gate_ref, tri_gain, tri_bias, out_w_ref,
    trans_gain, trans_bias, trans_in, trans_out,
    out_ref,
    flat, work, left_t, right_f, gate, part, own, tri, msg, wide,
    right_all, sum_send, sum_recv, upd_send, upd_recv,
    a_send, a_recv, b_send, b_recv, c_send, c_recv,
):
    rows, cols, channels = pair_ref.shape
    hidden = proj_ref.shape[1] // 4
    tokens = mask_ref.shape[1]
    total = rows * cols
    piece = cols // n_row
    ratio = cols // rows
    expansion = trans_out.shape[0]
    chunk = chunk_of(total)
    r = lax.axis_index("row")
    q = lax.axis_index("col")

    barrier = pltpu.get_barrier_semaphore()
    for d in range(1, n_row):
        pl.semaphore_signal(barrier, inc=1, device_id={"row": lax.rem(r + d, n_row)}, device_id_type=MESH)
    for d in range(1, n_col):
        pl.semaphore_signal(barrier, inc=1, device_id={"col": lax.rem(q + d, n_col)}, device_id_type=MESH)

    def over_chunks(step):
        if chunk == total:
            step(0)
        else:
            pl.loop(0, total // chunk)(lambda n: step(pl.multiple_of(n * chunk, 16)))

    for i in range(rows):
        flat[i * cols:(i + 1) * cols, :] = pair_ref[i].astype(f32)

    def pair_weight(base):
        spot = lax.broadcasted_iota(jnp.int32, (chunk, tokens), 0).astype(f32) + (
            jnp.asarray(base, jnp.int32).astype(f32))
        token = lax.broadcasted_iota(jnp.int32, (chunk, tokens), 1).astype(f32)
        row_of = jnp.floor((spot + 0.5) * (1.0 / cols))
        col_of = spot - row_of * cols
        first = (token == row_of + (r * rows).astype(f32)).astype(f32)
        second = (token == col_of + (q * cols).astype(f32)).astype(f32)
        picked = ((first + second) * mask_ref[...].astype(f32)).astype(bf16)
        both = jnp.dot(picked, jnp.ones((tokens, hidden), bf16), preferred_element_type=f32)
        return (both > 1.5).astype(f32)

    def project(base):
        at = pl.ds(base, chunk)
        normed = layer_norm(flat[at, :], norm_gain[...], norm_bias[...]).astype(bf16)
        weight = pair_weight(base)
        right = jnp.dot(normed, proj_ref[:, 2 * hidden:], preferred_element_type=f32)
        panel = weight * sigmoid(right[:, hidden:]) * right[:, :hidden]
        right_all[r, at, :] = panel.astype(bf16)

    def project_left(base):
        at = pl.ds(base, chunk)
        normed = layer_norm(flat[at, :], norm_gain[...], norm_bias[...]).astype(bf16)
        weight = pair_weight(base)
        left = jnp.dot(normed, proj_ref[:, :2 * hidden], preferred_element_type=f32)
        panel = weight * sigmoid(left[:, hidden:]) * left[:, :hidden]
        work[at, :] = panel.astype(bf16).astype(f32)
        gate[at, :] = sigmoid(jnp.dot(normed, gate_ref[...], preferred_element_type=f32))

    over_chunks(project)
    pl.semaphore_wait(barrier, n_row - 1 + n_col - 1)

    def right_copy(block, slot, peer):
        return pltpu.make_async_remote_copy(
            src_ref=right_all.at[block], dst_ref=right_all.at[block],
            send_sem=a_send.at[slot], recv_sem=a_recv.at[block],
            device_id={"row": peer}, device_id_type=MESH)

    @pl.loop(1, n_row)
    def _(step):
        right_copy(r, step, nearest(r, step, n_row)).start()

    over_chunks(project_left)
    for k in range(cols):
        left_t[k] = work[pl.ds(k, rows, stride=cols), :]

    def sum_copy(block, peer):
        return pltpu.make_async_remote_copy(
            src_ref=sum_send.at[block], dst_ref=sum_recv.at[q, block % ratio],
            send_sem=b_send.at[block], recv_sem=b_recv.at[q, block % ratio],
            device_id={"col": peer}, device_id_type=MESH)

    span = chunk_k = next(size for size in (20, 16, 10, 8, 5, 4, 2, 1) if cols % size == 0)

    def triangle(block):
        right_f[...] = right_all[block].astype(f32)

        @pl.loop(0, rows // piece)
        def _(part_j):
            def steps(base_k, sums):
                sums = list(sums)
                for k in range(chunk_k):
                    mine = left_t[base_k * span + k]
                    for j in range(piece):
                        place = (part_j * piece + j) * cols + base_k * span + k
                        sums[j] = sums[j] + mine * right_f[pl.ds(place, 1), :]
                return tuple(sums)
            sums = tuple(jnp.zeros((rows, hidden), f32) for _ in range(piece))
            if chunk_k == cols:
                sums = steps(0, sums)
            else:
                sums = lax.fori_loop(0, cols // chunk_k, steps, sums)
            for j in range(piece):
                part[pl.ds(part_j * piece + j, rows, stride=rows), :] = sums[j]

        owner = block // ratio

        @pl.when(owner == q)
        def _():
            own[block % ratio] = part[...]

        @pl.when(owner != q)
        def _():
            sum_send[block] = part[...].astype(bf16)
            sum_copy(block, owner).start()

    triangle(r)

    @pl.loop(1, n_row)
    def _(step):
        block = nearest(r, step, n_row)
        right_copy(block, step, block).wait_recv()
        triangle(block)

    for half in range(ratio):
        sums = own[half]
        for d in range(1, n_col):
            other = lax.rem(q + d, n_col)
            pltpu.make_async_remote_copy(
                src_ref=sum_send.at[0], dst_ref=sum_recv.at[other, half],
                send_sem=b_send.at[0], recv_sem=b_recv.at[other, half],
                device_id={"col": other}, device_id_type=MESH).wait_recv()
            sums = sums + sum_recv[other, half].astype(f32)
        if ratio == 1:
            tri[...] = sums
        else:
            part[...] = sums
            for i in range(rows):
                tri[i * cols + half * rows:i * cols + (half + 1) * rows, :] = part[i * rows:(i + 1) * rows, :]

    def update(base):
        at = pl.ds(base, chunk)
        normed = layer_norm(tri[at, :], tri_gain[...], tri_bias[...]).astype(bf16)
        branch = jnp.dot(normed, out_w_ref[...], preferred_element_type=f32)
        work[at, :] = flat[at, :] + gate[at, :] * branch

    over_chunks(update)

    def upd_copy(slot, place, peer):
        return pltpu.make_async_remote_copy(
            src_ref=upd_send.at[slot], dst_ref=upd_recv.at[place],
            send_sem=c_send.at[slot], recv_sem=c_recv.at[place],
            device_id={"row": peer}, device_id_type=MESH)

    msg[...] = jnp.zeros_like(msg)

    @pl.loop(0, n_row)
    def _(step):
        target = nearest(r, n_row - 1 - step, n_row)
        for j in range(piece):
            msg[j * rows:(j + 1) * rows, :] = work[pl.ds(target * piece + j, rows, stride=cols), :]

        @pl.when(target == r)
        def _():
            upd_recv[r] = msg[...].astype(bf16)

        @pl.when(target != r)
        def _():
            upd_send[target] = msg[...].astype(bf16)
            upd_copy(target, r, target).start()

    def transition(source):
        state = upd_recv[source].astype(f32)
        normed = layer_norm(state, trans_gain[...], trans_bias[...]).astype(bf16)
        inner = jnp.dot(normed, trans_in[...], preferred_element_type=f32)
        swish = inner[:, :expansion]
        active = (swish * sigmoid(swish) * inner[:, expansion:]).astype(bf16)
        result = state + jnp.dot(active, trans_out[...], preferred_element_type=f32)
        for j in range(piece):
            wide[pl.ds(j, rows, stride=8), :] = result[j * rows:(j + 1) * rows, :]
        out_ref[pl.ds(source * rows, rows), 0] = wide[...].reshape(rows, 8, channels)[:, :piece].astype(bf16)

    wide[...] = jnp.zeros_like(wide)
    transition(r)

    @pl.loop(1, n_row)
    def _(step):
        source = nearest(r, step, n_row)
        upd_copy(source, source, source).wait_recv()
        transition(source)

    @pl.loop(1, n_row)
    def _(step):
        peer = nearest(r, step, n_row)
        right_copy(r, step, peer).wait_send()
        upd_copy(peer, r, peer).wait_send()

    @pl.loop(0, n_row)
    def _(block):
        @pl.when(block // ratio != q)
        def _():
            sum_copy(block, block // ratio).wait_send()


def body(n_row, n_col, pair_state, token_mask, norm_gain, norm_bias, proj_weight, gate_weight,
         tri_gain, tri_bias, out_weight, trans_gain, trans_bias, trans_in, trans_out):
    rows, cols, channels = pair_state.shape
    hidden = proj_weight.shape[1] // 4
    piece = cols // n_row
    ratio = cols // rows
    padded = -(-piece * rows // 16) * 16
    flat = lambda count: pltpu.VMEM((count, hidden), f32)
    line = lambda values: values.reshape(1, -1)
    return pl.pallas_call(
        functools.partial(kernel, n_row, n_col),
        out_shape=jax.ShapeDtypeStruct((rows * n_row, 1, piece, channels), bf16),
        in_specs=[pl.BlockSpec(memory_space=pltpu.VMEM)] * 13,
        out_specs=pl.BlockSpec(memory_space=pltpu.VMEM),
        scratch_shapes=[
            flat(rows * cols), flat(rows * cols),
            pltpu.VMEM((cols, rows, hidden), f32),
            flat(rows * cols), flat(rows * cols), flat(rows * rows),
            pltpu.VMEM((ratio, rows * rows, hidden), f32),
            flat(rows * cols), flat(padded), flat(rows * 8),
            pltpu.VMEM((n_row, rows * cols, hidden), bf16),
            pltpu.VMEM((n_row, rows * rows, hidden), bf16),
            pltpu.VMEM((n_col, ratio, rows * rows, hidden), bf16),
            pltpu.VMEM((n_row, padded, channels), bf16),
            pltpu.VMEM((n_row, padded, channels), bf16),
            pltpu.SemaphoreType.DMA((n_row,)), pltpu.SemaphoreType.DMA((n_row,)),
            pltpu.SemaphoreType.DMA((n_row,)), pltpu.SemaphoreType.DMA((n_col, ratio)),
            pltpu.SemaphoreType.DMA((n_row,)), pltpu.SemaphoreType.DMA((n_row,)),
        ],
        compiler_params=pltpu.CompilerParams(
            collective_id=0, has_side_effects=True, vmem_limit_bytes=56 * 1024 * 1024),
    )(pair_state, line(token_mask), line(norm_gain), line(norm_bias), proj_weight, gate_weight,
      line(tri_gain), line(tri_bias), out_weight, line(trans_gain), line(trans_bias), trans_in, trans_out)


def solution(mesh):
    in_specs = (P(("groups", "row"), "col", None), P("groups")) + (P(),) * 11
    out_specs = P("groups", "col", "row", None)
    return jax.shard_map(
        functools.partial(body, mesh.shape["row"], mesh.shape["col"]),
        mesh=mesh, in_specs=in_specs, out_specs=out_specs, check_vma=False)
```

```python
import functools

import jax
import jax.numpy as jnp
from jax import lax
from jax.experimental import pallas as pl
from jax.experimental.pallas import tpu as pltpu
from jax.sharding import PartitionSpec as P

epsilon = 1e-05
MESH = pl.DeviceIdType.MESH
f32 = jnp.float32
bf16 = jnp.bfloat16


def layer_norm(values, gain, bias):
    center = jnp.mean(values, axis=-1, keepdims=True)
    moved = values - center
    spread = jnp.mean(jnp.square(moved), axis=-1, keepdims=True)
    return moved * lax.rsqrt(spread + epsilon) * gain + bias


def sigmoid(values):
    return 0.5 * jnp.tanh(0.5 * values) + 0.5


def chunk_of(total):
    return max(size for size in range(16, 513, 16) if total % size == 0)


def nearest(me, step, count):
    ends = jnp.minimum(me, count - 1 - me)
    between = jnp.where(step % 2 == 1, me + (step + 1) // 2, me - step // 2)
    outside = jnp.where(me <= count - 1 - me, step, count - 1 - step)
    return jnp.where(step <= 2 * ends, between, outside)


def kernel(
    n_row, n_col, group_i, group_j,
    pair_ref, mask_ref, norm_gain, norm_bias, proj_ref, tri_gain, tri_bias,
    trans_gain, trans_bias, gate_hbm, out_w_hbm, trans_in_hbm, trans_out_hbm,
    out_ref,
    flat, work, left_t, right_f, gate, part, own, tri, msg, wide,
    gate_ref, out_w_ref, trans_in, trans_out,
    state_send, state_recv, right_own, left_all, right_all, sum_send, sum_recv, upd_send, upd_recv,
    load_sem, state_sem, l_send, l_recv, r_send, r_recv, b_send, b_recv, c_send, c_recv,
):
    rows, cols, channels = pair_ref.shape
    hidden = proj_ref.shape[1] // 4
    tokens = mask_ref.shape[1]
    total = rows * cols
    piece = cols // n_row
    ratio = cols // rows
    expansion = trans_out.shape[0]
    chunk = chunk_of(total)
    r = lax.axis_index("row")
    q = lax.axis_index("col")
    g, h = r // group_i, r % group_i

    def holder(row_block, col_block):
        first = col_block * ratio
        row = row_block // group_i * group_i + first // group_j
        return row, (row_block % group_i * group_j + first % group_j) // ratio

    tile_row = g * group_i + q * ratio // group_j
    tile_col = (h * group_j + q * ratio % group_j) // ratio

    barrier = pltpu.get_barrier_semaphore()
    devices = n_row * n_col

    @pl.loop(1, devices)
    def _(d):
        place = (r * n_col + q + d) % devices
        pl.semaphore_signal(
            barrier, inc=1, device_id={"row": place // n_col, "col": place % n_col}, device_id_type=MESH)

    loads = [
        pltpu.make_async_copy(source, target, load_sem.at[n])
        for n, (source, target) in enumerate((
            (gate_hbm, gate_ref), (out_w_hbm, out_w_ref), (trans_in_hbm, trans_in), (trans_out_hbm, trans_out)))]
    for load in loads:
        load.start()

    def over_chunks(step):
        if chunk == total:
            step(0)
        else:
            pl.loop(0, total // chunk)(lambda n: step(pl.multiple_of(n * chunk, 16)))

    for i in range(rows):
        flat[i * cols:(i + 1) * cols, :] = pair_ref[i].astype(f32)

    def pair_weight(base):
        spot = lax.broadcasted_iota(jnp.int32, (chunk, tokens), 0).astype(f32) + (
            jnp.asarray(base, jnp.int32).astype(f32))
        token = lax.broadcasted_iota(jnp.int32, (chunk, tokens), 1).astype(f32)
        row_of = jnp.floor((spot + 0.5) * (1.0 / cols))
        col_of = spot - row_of * cols
        first = (token == row_of + (r * rows).astype(f32)).astype(f32)
        second = (token == col_of + (q * cols).astype(f32)).astype(f32)
        picked = ((first + second) * mask_ref[...].astype(f32)).astype(bf16)
        both = jnp.dot(picked, jnp.ones((tokens, hidden), bf16), preferred_element_type=f32)
        return (both > 1.5).astype(f32)

    def project(base):
        at = pl.ds(base, chunk)
        normed = layer_norm(flat[at, :], norm_gain[...], norm_bias[...]).astype(bf16)
        weight = pair_weight(base)
        both = jnp.dot(normed, proj_ref[...], preferred_element_type=f32)
        panel = weight * sigmoid(both[:, 3 * hidden:]) * both[:, 2 * hidden:3 * hidden]
        right_own[at, :] = panel.astype(bf16)
        panel = weight * sigmoid(both[:, hidden:2 * hidden]) * both[:, :hidden]
        left_all[h, at, :] = panel.astype(bf16)
        state_send[at, :] = flat[at, :].astype(bf16)

    over_chunks(project)
    keeps_right = r // group_j == h
    state_row, state_col = holder(r, q)
    keeps_state = jnp.logical_and(state_row == r, state_col == q)
    pl.semaphore_wait(barrier, devices - 1)

    def right_copy(target, source_slot):
        return pltpu.make_async_remote_copy(
            src_ref=right_own, dst_ref=right_all.at[source_slot],
            send_sem=r_send.at[target], recv_sem=r_recv.at[source_slot],
            device_id={"row": target * group_i + r // group_j}, device_id_type=MESH)

    def left_copy(peer, slot):
        return pltpu.make_async_remote_copy(
            src_ref=left_all.at[slot], dst_ref=left_all.at[slot],
            send_sem=l_send.at[peer], recv_sem=l_recv.at[slot],
            device_id={"row": g * group_i + peer}, device_id_type=MESH)

    state_copy = pltpu.make_async_remote_copy(
        src_ref=state_send, dst_ref=state_recv, send_sem=state_sem.at[0], recv_sem=state_sem.at[1],
        device_id={"row": state_row, "col": state_col}, device_id_type=MESH)

    @pl.loop(0, group_j)
    def _(target):
        @pl.when(target * group_i + r // group_j != r)
        def _():
            right_copy(target, r % group_j).start()

    @pl.loop(1, group_i)
    def _(d):
        left_copy((h + d) % group_i, h).start()

    @pl.when(jnp.logical_not(keeps_state))
    def _():
        state_copy.start()

    @pl.when(keeps_state)
    def _():
        state_recv[...] = state_send[...]

    @pl.when(keeps_right)
    def _():
        right_all[r % group_j] = right_own[...]

    def sum_copy(block, peer):
        return pltpu.make_async_remote_copy(
            src_ref=sum_send.at[block], dst_ref=sum_recv.at[q, block % ratio],
            send_sem=b_send.at[block], recv_sem=b_recv.at[q, block % ratio],
            device_id={"col": peer}, device_id_type=MESH)

    chunk_k = next(size for size in (20, 16, 10, 8, 5, 4, 2, 1) if cols % size == 0)

    def triangle(slot, block):
        right_f[...] = right_all[slot].astype(f32)

        @pl.loop(0, rows // piece)
        def _(part_j):
            def steps(base_k, sums):
                sums = list(sums)
                for k in range(chunk_k):
                    mine = left_t[base_k * chunk_k + k]
                    for j in range(piece):
                        place = (part_j * piece + j) * cols + base_k * chunk_k + k
                        sums[j] = sums[j] + mine * right_f[pl.ds(place, 1), :]
                return tuple(sums)
            sums = tuple(jnp.zeros((rows, hidden), f32) for _ in range(piece))
            if chunk_k == cols:
                sums = steps(0, sums)
            else:
                sums = lax.fori_loop(0, cols // chunk_k, steps, sums)
            for j in range(piece):
                part[pl.ds(part_j * piece + j, rows, stride=rows), :] = sums[j]

        owner = block // ratio

        @pl.when(owner == q)
        def _():
            own[block % ratio] = part[...]

        @pl.when(owner != q)
        def _():
            sum_send[block] = part[...].astype(bf16)
            sum_copy(block, owner).start()

    first_right = jnp.clip(r - h * group_j, 0, group_j - 1)

    @pl.loop(0, group_i)
    def _(d):
        left = (h + d) % group_i

        @pl.when(d > 0)
        def _():
            left_copy(left, left).wait_recv()

        work[...] = left_all[left].astype(f32)
        for k in range(cols):
            left_t[k] = work[pl.ds(k, rows, stride=cols), :]

        @pl.loop(0, group_j)
        def _(e):
            slot = (first_right + e) % group_j

            @pl.when(jnp.logical_and(d == 0, h * group_j + slot != r))
            def _():
                right_copy(0, slot).wait_recv()

            triangle(slot, left * group_j + slot)

    loads[0].wait()
    loads[1].wait()

    @pl.when(jnp.logical_not(keeps_state))
    def _():
        state_copy.wait_recv()

    def gates(base):
        at = pl.ds(base, chunk)
        state = state_recv[at, :].astype(f32)
        normed = layer_norm(state, norm_gain[...], norm_bias[...]).astype(bf16)
        gate[at, :] = sigmoid(jnp.dot(normed, gate_ref[...], preferred_element_type=f32))

    over_chunks(gates)

    for half in range(ratio):
        sums = own[half]
        for d in range(1, n_col):
            other = lax.rem(q + d, n_col)
            pltpu.make_async_remote_copy(
                src_ref=sum_send.at[0], dst_ref=sum_recv.at[other, half],
                send_sem=b_send.at[0], recv_sem=b_recv.at[other, half],
                device_id={"col": other}, device_id_type=MESH).wait_recv()
            sums = sums + sum_recv[other, half].astype(f32)
        if ratio == 1:
            tri[...] = sums
        else:
            part[...] = sums
            for i in range(rows):
                tri[i * cols + half * rows:i * cols + (half + 1) * rows, :] = part[i * rows:(i + 1) * rows, :]

    def update(base):
        at = pl.ds(base, chunk)
        normed = layer_norm(tri[at, :], tri_gain[...], tri_bias[...]).astype(bf16)
        branch = jnp.dot(normed, out_w_ref[...], preferred_element_type=f32)
        work[at, :] = state_recv[at, :].astype(f32) + gate[at, :] * branch

    over_chunks(update)

    def upd_copy(slot, place, peer_row, peer_col):
        return pltpu.make_async_remote_copy(
            src_ref=upd_send.at[slot], dst_ref=upd_recv.at[place],
            send_sem=c_send.at[slot], recv_sem=c_recv.at[place],
            device_id={"row": peer_row, "col": peer_col}, device_id_type=MESH)

    def stays(target):
        return jnp.logical_and(target == r, tile_col == q)

    msg[...] = jnp.zeros_like(msg)

    @pl.loop(0, n_row)
    def _(step):
        target = nearest(r, n_row - 1 - step, n_row)
        for j in range(piece):
            msg[j * rows:(j + 1) * rows, :] = work[pl.ds(target * piece + j, rows, stride=cols), :]

        @pl.when(stays(target))
        def _():
            upd_recv[tile_row] = msg[...].astype(bf16)

        @pl.when(jnp.logical_not(stays(target)))
        def _():
            upd_send[target] = msg[...].astype(bf16)
            upd_copy(target, tile_row, target, tile_col).start()

    loads[2].wait()
    loads[3].wait()

    def transition(source):
        state = upd_recv[source].astype(f32)
        normed = layer_norm(state, trans_gain[...], trans_bias[...]).astype(bf16)
        inner = jnp.dot(normed, trans_in[...], preferred_element_type=f32)
        swish = inner[:, :expansion]
        active = (swish * sigmoid(swish) * inner[:, expansion:]).astype(bf16)
        result = state + jnp.dot(active, trans_out[...], preferred_element_type=f32)
        for j in range(piece):
            wide[pl.ds(j, rows, stride=8), :] = result[j * rows:(j + 1) * rows, :]
        out_ref[pl.ds(source * rows, rows), 0] = wide[...].reshape(rows, 8, channels)[:, :piece].astype(bf16)

    wide[...] = jnp.zeros_like(wide)

    @pl.loop(0, n_row)
    def _(step):
        source = nearest(r, step, n_row)
        from_row, from_col = holder(source, q)

        @pl.when(jnp.logical_or(from_row != r, from_col != q))
        def _():
            upd_copy(source, source, from_row, from_col).wait_recv()

        transition(source)

    @pl.loop(0, n_row)
    def _(target):
        @pl.when(jnp.logical_not(stays(target)))
        def _():
            upd_copy(target, tile_row, target, tile_col).wait_send()

        @pl.when(target // ratio != q)
        def _():
            sum_copy(target, target // ratio).wait_send()

    @pl.loop(0, group_j)
    def _(target):
        @pl.when(target * group_i + r // group_j != r)
        def _():
            right_copy(target, r % group_j).wait_send()

    @pl.loop(1, group_i)
    def _(d):
        left_copy((h + d) % group_i, h).wait_send()

    @pl.when(jnp.logical_not(keeps_state))
    def _():
        state_copy.wait_send()


def body(n_row, n_col, pair_state, token_mask, norm_gain, norm_bias, proj_weight, gate_weight,
         tri_gain, tri_bias, out_weight, trans_gain, trans_bias, trans_in, trans_out):
    rows, cols, channels = pair_state.shape
    hidden = proj_weight.shape[1] // 4
    piece = cols // n_row
    ratio = cols // rows
    padded = -(-piece * rows // 16) * 16
    group_i = max(size for size in range(1, n_row + 1) if n_row % size == 0 and size * size <= n_row)
    group_j = n_row // group_i
    flat = lambda count: pltpu.VMEM((count, hidden), f32)
    half = lambda *shape: pltpu.VMEM(shape + (hidden,), bf16)
    line = lambda values: values.reshape(1, -1)
    sems = lambda *shape: pltpu.SemaphoreType.DMA(shape)
    return pl.pallas_call(
        functools.partial(kernel, n_row, n_col, group_i, group_j),
        out_shape=jax.ShapeDtypeStruct((rows * n_row, 1, piece, channels), bf16),
        in_specs=[pl.BlockSpec(memory_space=pltpu.VMEM)] * 9 + [pl.BlockSpec(memory_space=pl.ANY)] * 4,
        out_specs=pl.BlockSpec(memory_space=pltpu.VMEM),
        scratch_shapes=[
            flat(rows * cols), flat(rows * cols),
            pltpu.VMEM((cols, rows, hidden), f32),
            flat(rows * cols), flat(rows * cols), flat(rows * rows),
            pltpu.VMEM((ratio, rows * rows, hidden), f32),
            flat(rows * cols), flat(padded), flat(rows * 8),
            pltpu.VMEM(gate_weight.shape, bf16), pltpu.VMEM(out_weight.shape, bf16),
            pltpu.VMEM(trans_in.shape, bf16), pltpu.VMEM(trans_out.shape, bf16),
            half(rows * cols), half(rows * cols), half(rows * cols),
            half(group_i, rows * cols), half(group_j, rows * cols),
            half(n_row, rows * rows), half(n_col, ratio, rows * rows),
            half(n_row, padded), half(n_row, padded),
            sems(4), sems(2), sems(group_i), sems(group_i), sems(group_j), sems(group_j),
            sems(n_row), sems(n_col, ratio), sems(n_row), sems(n_row),
        ],
        compiler_params=pltpu.CompilerParams(
            collective_id=0, has_side_effects=True, vmem_limit_bytes=56 * 1024 * 1024),
    )(pair_state, line(token_mask), line(norm_gain), line(norm_bias), proj_weight,
      line(tri_gain), line(tri_bias), line(trans_gain), line(trans_bias),
      gate_weight, out_weight, trans_in, trans_out)


def solution(mesh):
    in_specs = (P(("groups", "row"), "col", None), P("groups")) + (P(),) * 11
    out_specs = P("groups", "col", "row", None)
    return jax.shard_map(
        functools.partial(body, mesh.shape["row"], mesh.shape["col"]),
        mesh=mesh, in_specs=in_specs, out_specs=out_specs, check_vma=False)
```

```python
import functools

import jax
import jax.numpy as jnp
from jax import lax
from jax.experimental import pallas as pl
from jax.experimental.pallas import tpu as pltpu
from jax.sharding import PartitionSpec as P

epsilon = 1e-05
MESH = pl.DeviceIdType.MESH
f32 = jnp.float32
bf16 = jnp.bfloat16


def layer_norm(values, gain, bias):
    center = jnp.mean(values, axis=-1, keepdims=True)
    moved = values - center
    spread = jnp.mean(jnp.square(moved), axis=-1, keepdims=True)
    return moved * lax.rsqrt(spread + epsilon) * gain + bias


def sigmoid(values):
    return 0.5 * jnp.tanh(0.5 * values) + 0.5


def chunk_of(total):
    return max(size for size in range(16, 513, 16) if total % size == 0)


def nearest(me, step, count):
    ends = jnp.minimum(me, count - 1 - me)
    between = jnp.where(step % 2 == 1, me + (step + 1) // 2, me - step // 2)
    outside = jnp.where(me <= count - 1 - me, step, count - 1 - step)
    return jnp.where(step <= 2 * ends, between, outside)


def kernel(
    n_row, n_col, group_i, group_j,
    pair_ref, mask_ref, norm_gain, norm_bias, proj_ref, tri_gain, tri_bias,
    trans_gain, trans_bias, gate_hbm, out_w_hbm, trans_in_hbm, trans_out_hbm,
    out_ref,
    flat, work, left_t, right_f, gate, part, own, tri, msg, wide,
    gate_ref, out_w_ref, trans_in, trans_out,
    state_send, state_recv, right_own, left_all, right_all, sum_send, sum_recv, upd_send, upd_recv,
    load_sem, state_sem, l_send, l_recv, r_send, r_recv, b_send, b_recv, c_send, c_recv,
):
    rows, cols, channels = pair_ref.shape
    hidden = proj_ref.shape[1] // 4
    tokens = mask_ref.shape[1]
    total = rows * cols
    piece = cols // n_row
    ratio = cols // rows
    expansion = trans_out.shape[0]
    chunk = chunk_of(total)
    r = lax.axis_index("row")
    q = lax.axis_index("col")
    g, h = r // group_i, r % group_i

    def holder(row_block, col_block):
        first = col_block * ratio
        row = row_block // group_i * group_i + first // group_j
        return row, (row_block % group_i * group_j + first % group_j) // ratio

    tile_row = g * group_i + q * ratio // group_j
    tile_col = (h * group_j + q * ratio % group_j) // ratio

    barrier = pltpu.get_barrier_semaphore()
    devices = n_row * n_col

    @pl.loop(1, devices)
    def _(d):
        place = (r * n_col + q + d) % devices
        pl.semaphore_signal(
            barrier, inc=1, device_id={"row": place // n_col, "col": place % n_col}, device_id_type=MESH)

    loads = [
        pltpu.make_async_copy(source, target, load_sem.at[n])
        for n, (source, target) in enumerate((
            (gate_hbm, gate_ref), (out_w_hbm, out_w_ref), (trans_in_hbm, trans_in), (trans_out_hbm, trans_out)))]
    for load in loads:
        load.start()

    def over_chunks(step):
        if chunk == total:
            step(0)
        else:
            pl.loop(0, total // chunk)(lambda n: step(pl.multiple_of(n * chunk, 16)))

    for i in range(rows):
        flat[i * cols:(i + 1) * cols, :] = pair_ref[i].astype(f32)

    def pair_weight(base):
        spot = lax.broadcasted_iota(jnp.int32, (chunk, tokens), 0).astype(f32) + (
            jnp.asarray(base, jnp.int32).astype(f32))
        token = lax.broadcasted_iota(jnp.int32, (chunk, tokens), 1).astype(f32)
        row_of = jnp.floor((spot + 0.5) * (1.0 / cols))
        col_of = spot - row_of * cols
        first = (token == row_of + (r * rows).astype(f32)).astype(f32)
        second = (token == col_of + (q * cols).astype(f32)).astype(f32)
        picked = ((first + second) * mask_ref[...].astype(f32)).astype(bf16)
        both = jnp.dot(picked, jnp.ones((tokens, hidden), bf16), preferred_element_type=f32)
        return (both > 1.5).astype(f32)

    def project(base):
        at = pl.ds(base, chunk)
        normed = layer_norm(flat[at, :], norm_gain[...], norm_bias[...]).astype(bf16)
        weight = pair_weight(base)
        both = jnp.dot(normed, proj_ref[...], preferred_element_type=f32)
        panel = weight * sigmoid(both[:, 3 * hidden:]) * both[:, 2 * hidden:3 * hidden]
        right_own[at, :] = panel.astype(bf16)
        panel = weight * sigmoid(both[:, hidden:2 * hidden]) * both[:, :hidden]
        left_all[h, at, :] = panel.astype(bf16)
        state_send[at, :] = flat[at, :].astype(bf16)

    over_chunks(project)
    keeps_right = r // group_j == h
    state_row, state_col = holder(r, q)
    keeps_state = jnp.logical_and(state_row == r, state_col == q)
    pl.semaphore_wait(barrier, devices - 1)

    def right_copy(target, source_slot):
        return pltpu.make_async_remote_copy(
            src_ref=right_own, dst_ref=right_all.at[source_slot],
            send_sem=r_send.at[target], recv_sem=r_recv.at[source_slot],
            device_id={"row": target * group_i + r // group_j}, device_id_type=MESH)

    def left_copy(peer, slot):
        return pltpu.make_async_remote_copy(
            src_ref=left_all.at[slot], dst_ref=left_all.at[slot],
            send_sem=l_send.at[peer], recv_sem=l_recv.at[slot],
            device_id={"row": g * group_i + peer}, device_id_type=MESH)

    state_copy = pltpu.make_async_remote_copy(
        src_ref=state_send, dst_ref=state_recv, send_sem=state_sem.at[0], recv_sem=state_sem.at[1],
        device_id={"row": state_row, "col": state_col}, device_id_type=MESH)

    @pl.loop(1, group_i)
    def _(d):
        left_copy((h + d) % group_i, h).start()

    @pl.loop(0, group_j)
    def _(target):
        @pl.when(target * group_i + r // group_j != r)
        def _():
            right_copy(target, r % group_j).start()

    @pl.when(jnp.logical_not(keeps_state))
    def _():
        state_copy.start()

    @pl.when(keeps_state)
    def _():
        state_recv[...] = state_send[...]

    @pl.when(keeps_right)
    def _():
        right_all[r % group_j] = right_own[...]

    def sum_copy(block, peer):
        return pltpu.make_async_remote_copy(
            src_ref=sum_send.at[block], dst_ref=sum_recv.at[q, block % ratio],
            send_sem=b_send.at[block], recv_sem=b_recv.at[q, block % ratio],
            device_id={"col": peer}, device_id_type=MESH)

    chunk_k = next(size for size in (20, 16, 10, 8, 5, 4, 2, 1) if cols % size == 0)

    def triangle(left, block):
        @pl.loop(0, rows // piece)
        def _(part_j):
            def steps(base_k, sums):
                sums = list(sums)
                for k in range(chunk_k):
                    mine = left_t[left, base_k * chunk_k + k]
                    for j in range(piece):
                        place = (part_j * piece + j) * cols + base_k * chunk_k + k
                        sums[j] = sums[j] + mine * right_f[pl.ds(place, 1), :]
                return tuple(sums)
            sums = tuple(jnp.zeros((rows, hidden), f32) for _ in range(piece))
            if chunk_k == cols:
                sums = steps(0, sums)
            else:
                sums = lax.fori_loop(0, cols // chunk_k, steps, sums)
            for j in range(piece):
                part[pl.ds(part_j * piece + j, rows, stride=rows), :] = sums[j]

        owner = block // ratio

        @pl.when(owner == q)
        def _():
            own[block % ratio] = part[...]

        @pl.when(owner != q)
        def _():
            sum_send[block] = part[...].astype(bf16)
            sum_copy(block, owner).start()

    first_right = jnp.clip(r - h * group_j, 0, group_j - 1)

    @pl.loop(0, group_j)
    def _(e):
        slot = (first_right + e) % group_j

        @pl.when(h * group_j + slot != r)
        def _():
            right_copy(0, slot).wait_recv()

        right_f[...] = right_all[slot].astype(f32)

        @pl.loop(0, group_i)
        def _(d):
            left = jnp.where(e == 0, h + d, q * group_i // n_col + 1 + d) % group_i

            @pl.when(jnp.logical_and(e == 0, d > 0))
            def _():
                left_copy(left, left).wait_recv()

            @pl.when(e == 0)
            def _():
                work[...] = left_all[left].astype(f32)
                for k in range(cols):
                    left_t[left, k] = work[pl.ds(k, rows, stride=cols), :]

            triangle(left, left * group_j + slot)

    loads[0].wait()
    loads[1].wait()

    @pl.when(jnp.logical_not(keeps_state))
    def _():
        state_copy.wait_recv()

    def gates(base):
        at = pl.ds(base, chunk)
        state = state_recv[at, :].astype(f32)
        normed = layer_norm(state, norm_gain[...], norm_bias[...]).astype(bf16)
        gate[at, :] = sigmoid(jnp.dot(normed, gate_ref[...], preferred_element_type=f32))

    over_chunks(gates)

    for half in range(ratio):
        sums = own[half]
        for d in range(1, n_col):
            other = lax.rem(q + d, n_col)
            pltpu.make_async_remote_copy(
                src_ref=sum_send.at[0], dst_ref=sum_recv.at[other, half],
                send_sem=b_send.at[0], recv_sem=b_recv.at[other, half],
                device_id={"col": other}, device_id_type=MESH).wait_recv()
            sums = sums + sum_recv[other, half].astype(f32)
        if ratio == 1:
            tri[...] = sums
        else:
            part[...] = sums
            for i in range(rows):
                tri[i * cols + half * rows:i * cols + (half + 1) * rows, :] = part[i * rows:(i + 1) * rows, :]

    def update(base):
        at = pl.ds(base, chunk)
        normed = layer_norm(tri[at, :], tri_gain[...], tri_bias[...]).astype(bf16)
        branch = jnp.dot(normed, out_w_ref[...], preferred_element_type=f32)
        work[at, :] = state_recv[at, :].astype(f32) + gate[at, :] * branch

    over_chunks(update)

    def upd_copy(slot, place, peer_row, peer_col):
        return pltpu.make_async_remote_copy(
            src_ref=upd_send.at[slot], dst_ref=upd_recv.at[place],
            send_sem=c_send.at[slot], recv_sem=c_recv.at[place],
            device_id={"row": peer_row, "col": peer_col}, device_id_type=MESH)

    def stays(target):
        return jnp.logical_and(target == r, tile_col == q)

    msg[...] = jnp.zeros_like(msg)

    @pl.loop(0, n_row)
    def _(step):
        target = nearest(r, n_row - 1 - step, n_row)
        for j in range(piece):
            msg[j * rows:(j + 1) * rows, :] = work[pl.ds(target * piece + j, rows, stride=cols), :]

        @pl.when(stays(target))
        def _():
            upd_recv[tile_row] = msg[...].astype(bf16)

        @pl.when(jnp.logical_not(stays(target)))
        def _():
            upd_send[target] = msg[...].astype(bf16)
            upd_copy(target, tile_row, target, tile_col).start()

    loads[2].wait()
    loads[3].wait()

    def transition(source):
        state = upd_recv[source].astype(f32)
        normed = layer_norm(state, trans_gain[...], trans_bias[...]).astype(bf16)
        inner = jnp.dot(normed, trans_in[...], preferred_element_type=f32)
        swish = inner[:, :expansion]
        active = (swish * sigmoid(swish) * inner[:, expansion:]).astype(bf16)
        result = state + jnp.dot(active, trans_out[...], preferred_element_type=f32)
        for j in range(piece):
            wide[pl.ds(j, rows, stride=8), :] = result[j * rows:(j + 1) * rows, :]
        out_ref[pl.ds(source * rows, rows), 0] = wide[...].reshape(rows, 8, channels)[:, :piece].astype(bf16)

    wide[...] = jnp.zeros_like(wide)

    @pl.loop(0, n_row)
    def _(step):
        source = nearest(r, step, n_row)
        from_row, from_col = holder(source, q)

        @pl.when(jnp.logical_or(from_row != r, from_col != q))
        def _():
            upd_copy(source, source, from_row, from_col).wait_recv()

        transition(source)

    @pl.loop(0, n_row)
    def _(target):
        @pl.when(jnp.logical_not(stays(target)))
        def _():
            upd_copy(target, tile_row, target, tile_col).wait_send()

        @pl.when(target // ratio != q)
        def _():
            sum_copy(target, target // ratio).wait_send()

    @pl.loop(0, group_j)
    def _(target):
        @pl.when(target * group_i + r // group_j != r)
        def _():
            right_copy(target, r % group_j).wait_send()

    @pl.loop(1, group_i)
    def _(d):
        left_copy((h + d) % group_i, h).wait_send()

    @pl.when(jnp.logical_not(keeps_state))
    def _():
        state_copy.wait_send()


def body(n_row, n_col, pair_state, token_mask, norm_gain, norm_bias, proj_weight, gate_weight,
         tri_gain, tri_bias, out_weight, trans_gain, trans_bias, trans_in, trans_out):
    rows, cols, channels = pair_state.shape
    hidden = proj_weight.shape[1] // 4
    piece = cols // n_row
    ratio = cols // rows
    padded = -(-piece * rows // 16) * 16
    group_i = max(size for size in range(1, n_row + 1) if n_row % size == 0 and size * size <= n_row)
    group_j = n_row // group_i
    flat = lambda count: pltpu.VMEM((count, hidden), f32)
    half = lambda *shape: pltpu.VMEM(shape + (hidden,), bf16)
    line = lambda values: values.reshape(1, -1)
    sems = lambda *shape: pltpu.SemaphoreType.DMA(shape)
    return pl.pallas_call(
        functools.partial(kernel, n_row, n_col, group_i, group_j),
        out_shape=jax.ShapeDtypeStruct((rows * n_row, 1, piece, channels), bf16),
        in_specs=[pl.BlockSpec(memory_space=pltpu.VMEM)] * 9 + [pl.BlockSpec(memory_space=pl.ANY)] * 4,
        out_specs=pl.BlockSpec(memory_space=pltpu.VMEM),
        scratch_shapes=[
            flat(rows * cols), flat(rows * cols),
            pltpu.VMEM((group_i, cols, rows, hidden), f32),
            flat(rows * cols), flat(rows * cols), flat(rows * rows),
            pltpu.VMEM((ratio, rows * rows, hidden), f32),
            flat(rows * cols), flat(padded), flat(rows * 8),
            pltpu.VMEM(gate_weight.shape, bf16), pltpu.VMEM(out_weight.shape, bf16),
            pltpu.VMEM(trans_in.shape, bf16), pltpu.VMEM(trans_out.shape, bf16),
            half(rows * cols), half(rows * cols), half(rows * cols),
            half(group_i, rows * cols), half(group_j, rows * cols),
            half(n_row, rows * rows), half(n_col, ratio, rows * rows),
            half(n_row, padded), half(n_row, padded),
            sems(4), sems(2), sems(group_i), sems(group_i), sems(group_j), sems(group_j),
            sems(n_row), sems(n_col, ratio), sems(n_row), sems(n_row),
        ],
        compiler_params=pltpu.CompilerParams(
            collective_id=0, has_side_effects=True, vmem_limit_bytes=56 * 1024 * 1024),
    )(pair_state, line(token_mask), line(norm_gain), line(norm_bias), proj_weight,
      line(tri_gain), line(tri_bias), line(trans_gain), line(trans_bias),
      gate_weight, out_weight, trans_in, trans_out)


def solution(mesh):
    in_specs = (P(("groups", "row"), "col", None), P("groups")) + (P(),) * 11
    out_specs = P("groups", "col", "row", None)
    return jax.shard_map(
        functools.partial(body, mesh.shape["row"], mesh.shape["col"]),
        mesh=mesh, in_specs=in_specs, out_specs=out_specs, check_vma=False)
```
